128 devices in a mesh: grp: 16 (over z, x_lo, core), col: 8 (over x_hi, y).
Axes of the slice: x: 4 (x_hi: 2, x_lo: 2; x = x_hi * 2 + x_lo), y: 4, z: 4, core: 2. Of those that a mesh axis runs over, the one named last changes fastest.
Arguments:
- constraint_rows: float32 [4096, 16384], P('grp', 'col'), may hold values from -0.125 to 0.125
- shift: float32 [16384], P('col'), may hold values from 0.3 to 1
- group_rows: int32 [16], replicated, may hold values from 1 to 256, 2048 in all
- panel_index: int32 [1], replicated, may hold values from 0 to 31
Outputs:
- panel_factor: float32 [16384, 512], P(('col', 'grp'))
The draws below stay inside these ranges and needn't reach their ends.
Inputs may be any that keep to these rules, and one draw needn't show every extreme that they name: `group_rows`: the values sum to 2048 and the largest equals 256.
All inputs are finite; a program needn't handle non-finite values.
Results may differ from the reference program's by a relative error of at most 0.000076.
Values sent between devices are 32-bit elements; how exact they have to be, the bound alone decides.
A program may use at most 64 MiB of HBM per device.

```python
import math
import jax
import jax.numpy as jnp
import numpy as np
from jax import lax

NQ = 16384
PANEL = 512
GROUP_ROWS = 256
ALL_ROWS = 4096
N_GRP = 16


def shard_levels(key, shape, shards, smallest, top_value):
    level, own = 1.0, jax.random.fold_in(key, 6)
    for axis_at, blocks in shards:
        heights = jnp.exp(jax.random.uniform(jax.random.fold_in(own, axis_at), (blocks,), jnp.float32, smallest / len(shards), top_value / len(shards)))
        level = level * jnp.repeat(heights, shape[axis_at] // blocks).reshape([-1 if axis == axis_at else 1 for axis in range(len(shape))])
    return level


def profile(count, total, reach, skew):
    portions = [(1 << 20) // math.isqrt(grade ** skew) + 1 for grade in range(2, count + 1)]
    surplus, holding = total - reach - (count - 1), [1] * (count - 1)
    while surplus > 0:
        movable = [i for i in range(count - 1) if holding[i] < reach]
        pool, left = sum([portions[i] for i in movable]), surplus
        for i in movable:
            addition = min(reach - holding[i], max(1, left * portions[i] // pool), surplus)
            holding[i] = holding[i] + addition
            surplus = surplus - addition
    return np.array([reach] + holding)


def ragged(own_key, number_of, total, reach, lean):
    if number_of == 2:
        one = jax.random.randint(own_key, (), max(1, total - reach), min(reach, total - 1) + 1)
        return jnp.stack([one, total - one])
    tallies = jnp.asarray(profile(number_of, total, reach, lean), jnp.int32)
    pairs = (number_of - 1) // 2
    source_of, taker = tallies[1:1 + 2 * pairs:2], tallies[2:2 + 2 * pairs:2]
    slack = jnp.minimum(source_of - 1, reach - taker)
    shifted = jax.random.randint(jax.random.fold_in(own_key, 1), (pairs,), 0, 1 << 20) % (slack + 1)
    tallies = tallies.at[1:1 + 2 * pairs:2].set(source_of - shifted).at[2:2 + 2 * pairs:2].set(taker + shifted)
    return tallies[jax.random.permutation(jax.random.fold_in(own_key, 2), number_of)]


def gaussian(stream_key, shape, scale, bound, pieces=(), kind=jnp.bfloat16):
    drawn = jax.random.normal(stream_key, shape, jnp.float32) * scale
    if len(pieces) > 0:
        drawn = shard_levels(stream_key, shape, pieces, -0.22, 0.18) * drawn
    return jnp.clip(drawn, min=-bound, max=bound).astype(kind)


def setup_inputs(seed: int = 0) -> dict:
    splits = jax.random.split(jax.random.key(seed), 5)
    return {
        "constraint_rows": gaussian(splits[0], (ALL_ROWS, NQ), (ALL_ROWS // 2) ** -0.5, 0.125, ((0, 16), (1, 8)), jnp.float32),
        "shift": jnp.clip(0.3 + 0.7 * jax.random.uniform(splits[1], (NQ,), jnp.float32) ** shard_levels(splits[1], (NQ,), ((0, 8),), -0.2, 0.2), 0.3, 1.0),
        "group_rows": ragged(splits[2], N_GRP, ALL_ROWS // 2, GROUP_ROWS, 2).astype(jnp.int32),
        "panel_index": jax.random.randint(splits[3], (1,), 0, NQ // PANEL).astype(jnp.int32),
    }


def reference(constraint_rows, shift, group_rows, panel_index):
    start = panel_index[0].astype(jnp.int32) * PANEL
    rows = jnp.arange(ALL_ROWS, dtype=jnp.int32)
    counts = group_rows[rows // GROUP_ROWS]
    live = rows % GROUP_ROWS < counts
    panel_cols = lax.dynamic_slice_in_dim(constraint_rows, start, PANEL, 1)
    panel_cols = jnp.where(live[:, None], panel_cols, jnp.zeros_like(panel_cols))
    schur_panel = lax.dot_general(constraint_rows.astype(jnp.float32), panel_cols.astype(jnp.float32), (((0,), (0,)), ((), ())), precision=lax.Precision.HIGHEST, preferred_element_type=jnp.float32)
    index_rows = jnp.arange(NQ, dtype=jnp.int32)
    index_cols = jnp.arange(PANEL, dtype=jnp.int32)
    on_diag = index_rows[:, None] == start + index_cols[None, :]
    schur_panel = schur_panel + jnp.where(on_diag, shift[:, None], jnp.zeros_like(schur_panel))
    block = lax.dynamic_slice_in_dim(schur_panel, start, PANEL, 0)
    factor = jnp.linalg.cholesky(block)
    return lax.linalg.triangular_solve(factor, schur_panel, left_side=False, lower=True, transpose_a=True)
```

```python
import jax, jax.numpy as jnp
from jax import lax
from jax.experimental import pallas as pl
from jax.experimental.pallas import tpu as pltpu

from jax.sharding import PartitionSpec as P

PANEL = 512


B = 128
HI = lax.Precision.HIGHEST


def inv_chol(rows):
    lane = lax.broadcasted_iota(jnp.int32, (8, B), 1)
    rows = list(rows)
    for s in range(16):
        k0 = 8 * s
        inside = (lane >= k0) & (lane < k0 + 8)
        tile = rows[s]
        spread = lambda t, l: jnp.broadcast_to(t[:, k0 + l : k0 + l + 1], (8, B))
        cols = [spread(tile, l) for l in range(8)]
        c = {(m, l): jnp.broadcast_to(cols[l][m : m + 1, :], (8, B)) for l in range(8) for m in range(l, 8)}
        r = [
            jnp.where(inside, jnp.where(lane == k0 + m, 1.0, 0.0), jnp.broadcast_to(tile[m : m + 1, :], (8, B)))
            for m in range(8)
        ]
        rs, low = {}, {}
        for j in range(8):
            rs[j] = lax.rsqrt(c[j, j])
            r[j] = r[j] * rs[j]
            for m in range(j + 1, 8):
                low[m, j] = c[m, j] * rs[j]
            for m in range(j + 1, 8):
                for n in range(j + 1, m + 1):
                    c[m, n] = c[m, n] - low[m, j] * low[n, j]
                r[m] = r[m] - low[m, j] * r[j]
        sub = lax.broadcasted_iota(jnp.int32, (8, B), 0)
        done = r[0]
        for j in range(1, 8):
            done = jnp.where(sub == j, r[j], done)
        rows[s] = jnp.where(lane < k0 + 8, done, 0.0)
        if s < 15:
            g = list(r)
            for j in reversed(range(8)):
                for m in range(j + 1, 8):
                    g[j] = g[j] - low[m, j] * g[m]
                g[j] = g[j] * rs[j]
            for i in range(s + 1, 16):
                f = [spread(rows[i], l) for l in range(8)]
                t = jnp.where(inside, 0.0, rows[i])
                p0 = f[0] * g[0] + f[1] * g[1]
                p1 = f[2] * g[2] + f[3] * g[3]
                p2 = f[4] * g[4] + f[5] * g[5]
                p3 = f[6] * g[6] + f[7] * g[7]
                rows[i] = t - ((p0 + p1) + (p2 + p3))
    return rows


def dot(a, b, dims=((1,), (0,))):
    return lax.dot_general(a, b, (dims, ((), ())), precision=HI, preferred_element_type=jnp.float32)


def factor_and_solve(m_ref, blocks):
    n = blocks * B
    width = m_ref.shape[1]
    for k in range(blocks):
        at = k * B
        w = jnp.concatenate(inv_chol([m_ref[at + 8 * i : at + 8 * i + 8, at : at + B] for i in range(16)]), axis=0)
        u = dot(w, m_ref[at : at + B, at + B :])
        if k == blocks - 1:
            return u
        m_ref[at : at + B, at + B :] = u
        for r in range(k + 1, blocks):
            left = u[:, (r - k - 1) * B : (r - k) * B]
            m_ref[r * B : (r + 1) * B, r * B :] -= dot(left, u[:, (r - k - 1) * B :], ((0,), (0,)))


def solve_kernel(d_ref, t_ref, x_ref, m_ref):
    n = d_ref.shape[0]
    m_ref[:, :n] = d_ref[...]
    m_ref[:, n:] = t_ref[...]
    blocks = n // B
    last = factor_and_solve(m_ref, blocks)
    for k in range(blocks):
        block = last if k == blocks - 1 else m_ref[k * B : (k + 1) * B, n:]
        x_ref[:, k * B : (k + 1) * B] = block.T


def solve(d, t):
    n, w = d.shape[0], t.shape[1]
    return pl.pallas_call(
        solve_kernel,
        out_shape=jax.ShapeDtypeStruct((w, n), jnp.float32),
        scratch_shapes=[pltpu.VMEM((n, n + w), jnp.float32)],
        compiler_params=pltpu.CompilerParams(vmem_limit_bytes=32 << 20),
    )(d, t)


def picked(x, axis, root):
    return lax.dynamic_index_in_dim(lax.all_gather(x, axis), root, 0, keepdims=False)


def cut_along(x, dim, size):
    before, after = (x.shape[:dim], x.shape[dim + 1 :])
    return jnp.moveaxis(x.reshape(*before, size, -1, *after), dim, 0)


def sent_and_summed(x, axis, dim):
    pieces = cut_along(x, dim, lax.axis_size(axis))
    arrived = lax.all_to_all(pieces, axis, split_axis=0, concat_axis=0, tiled=True)
    return arrived.sum(axis=0)


def product(left, right):
    return lax.dot_general(
        left,
        right,
        (((0,), (0,)), ((), ())),
        precision=lax.Precision.HIGHEST,
        preferred_element_type=jnp.float32,
    )


def gram_rows(left, panel_cols):
    return product(left, panel_cols)


def add_shift(values, shift_part, first_row, start):
    row_ids = first_row + jnp.arange(values.shape[0], dtype=jnp.int32)
    col_ids = jnp.arange(values.shape[1], dtype=jnp.int32)
    on_diag = row_ids[:, None] == start + col_ids[None, :]
    return values + jnp.where(on_diag, shift_part[:, None], jnp.zeros_like(values))


def on_device(constraint_rows, shift, group_rows, panel_index):
    width = constraint_rows.shape[1]
    groups = lax.axis_size("grp")
    col_idx = lax.axis_index("col")
    grp_idx = lax.axis_index("grp")
    share = width // groups
    start = panel_index[0] * PANEL
    owner = start // width
    local = start - owner * width
    live_count = lax.dynamic_index_in_dim(group_rows, grp_idx, keepdims=False)
    row_ids = jnp.arange(constraint_rows.shape[0], dtype=jnp.int32)
    masked = jnp.where(
        (row_ids < live_count)[:, None], constraint_rows, jnp.zeros_like(constraint_rows)
    )
    own_cols = lax.dynamic_slice_in_dim(masked, local, PANEL, 1)
    panel_cols = picked(own_cols, "col", owner)
    mine = sent_and_summed(gram_rows(masked, panel_cols), "grp", 0)
    shift_part = lax.dynamic_slice_in_dim(shift, grp_idx * share, share, 0)
    mine = add_shift(mine, shift_part, col_idx * width + grp_idx * share, start)
    from_owner = picked(mine, "col", owner)
    owner_shard = lax.all_gather(from_owner, "grp", axis=0, tiled=True)
    block = lax.dynamic_slice_in_dim(owner_shard, local, PANEL, 0)
    return solve(block, mine.T)


def solution(mesh):
    placed = (P("grp", "col"), P("col"), P(), P())
    return jax.shard_map(
        on_device, mesh=mesh, in_specs=placed, out_specs=P(("col", "grp"), None), check_vma=False
    )
```

```python
import jax, jax.numpy as jnp
from jax import lax
from jax.experimental import pallas as pl
from jax.experimental.pallas import tpu as pltpu
from jax.sharding import PartitionSpec as P

B = 128
HI = lax.Precision.HIGHEST


def inv_chol(rows):
    lane = lax.broadcasted_iota(jnp.int32, (8, B), 1)
    rows = list(rows)
    for s in range(16):
        k0 = 8 * s
        inside = (lane >= k0) & (lane < k0 + 8)
        tile = rows[s]
        spread = lambda t, l: jnp.broadcast_to(t[:, k0 + l : k0 + l + 1], (8, B))
        cols = [spread(tile, l) for l in range(8)]
        c = {(m, l): jnp.broadcast_to(cols[l][m : m + 1, :], (8, B)) for l in range(8) for m in range(l, 8)}
        r = [
            jnp.where(inside, jnp.where(lane == k0 + m, 1.0, 0.0), jnp.broadcast_to(tile[m : m + 1, :], (8, B)))
            for m in range(8)
        ]
        rs, low = {}, {}
        for j in range(8):
            rs[j] = lax.rsqrt(c[j, j])
            r[j] = r[j] * rs[j]
            for m in range(j + 1, 8):
                low[m, j] = c[m, j] * rs[j]
            for m in range(j + 1, 8):
                for n in range(j + 1, m + 1):
                    c[m, n] = c[m, n] - low[m, j] * low[n, j]
                r[m] = r[m] - low[m, j] * r[j]
        sub = lax.broadcasted_iota(jnp.int32, (8, B), 0)
        done = r[0]
        for j in range(1, 8):
            done = jnp.where(sub == j, r[j], done)
        rows[s] = jnp.where(lane < k0 + 8, done, 0.0)
        if s < 15:
            g = list(r)
            for j in reversed(range(8)):
                for m in range(j + 1, 8):
                    g[j] = g[j] - low[m, j] * g[m]
                g[j] = g[j] * rs[j]
            for i in range(s + 1, 16):
                f = [spread(rows[i], l) for l in range(8)]
                t = jnp.where(inside, 0.0, rows[i])
                p0 = f[0] * g[0] + f[1] * g[1]
                p1 = f[2] * g[2] + f[3] * g[3]
                p2 = f[4] * g[4] + f[5] * g[5]
                p3 = f[6] * g[6] + f[7] * g[7]
                rows[i] = t - ((p0 + p1) + (p2 + p3))
    return rows


def dot(a, b, dims=((1,), (0,))):
    return lax.dot_general(a, b, (dims, ((), ())), precision=HI, preferred_element_type=jnp.float32)


def factor_and_solve(m_ref, blocks):
    n = blocks * B
    width = m_ref.shape[1]
    for k in range(blocks):
        at = k * B
        w = jnp.concatenate(inv_chol([m_ref[at + 8 * i : at + 8 * i + 8, at : at + B] for i in range(16)]), axis=0)
        u = dot(w, m_ref[at : at + B, at + B :])
        if k == blocks - 1:
            return u
        m_ref[at : at + B, at + B :] = u
        for r in range(k + 1, blocks):
            left = u[:, (r - k - 1) * B : (r - k) * B]
            m_ref[r * B : (r + 1) * B, r * B :] -= dot(left, u[:, (r - k - 1) * B :], ((0,), (0,)))


def solve_kernel(d_ref, t_ref, x_ref, m_ref):
    n, w = t_ref.shape
    blocks = n // B
    for k in range(blocks):
        m_ref[k * B : (k + 1) * B, k * B : n] = d_ref[:, OFFSETS[k] : OFFSETS[k] + n - k * B]
    m_ref[:, n:] = t_ref[...]
    last = factor_and_solve(m_ref, blocks)
    for k in range(blocks):
        block = last if k == blocks - 1 else m_ref[k * B : (k + 1) * B, n:]
        x_ref[:, k * B : (k + 1) * B] = block.T


def solve(d, t):
    n, w = t.shape
    return pl.pallas_call(
        solve_kernel,
        out_shape=jax.ShapeDtypeStruct((w, n), jnp.float32),
        scratch_shapes=[pltpu.VMEM((n, n + w), jnp.float32)],
        compiler_params=pltpu.CompilerParams(vmem_limit_bytes=32 << 20),
    )(d, t)


GROUP_ROWS = 256
WIDTH = 2048
PANEL = 512
CHIPS = 8
COLS = 8
PIECE = GROUP_ROWS // COLS
SHARE = 128
OFFSETS = [0, 512, 896, 1152]
PACKED = 1280
MESH = pl.DeviceIdType.MESH


def where_am_i():
    grp, col = lax.axis_index("grp"), lax.axis_index("col")
    return grp, col, lax.rem(grp, 2), grp // 2


def chip_peer(chip, step):
    z = lax.rem(chip // 2 + step // 2, 4)
    x = lax.rem(lax.rem(chip, 2) + step % 2, 2)
    return z * 2 + x


def col_peer(col, step):
    x = lax.rem(col // 4 + step // 4, 2)
    y = lax.rem(lax.rem(col, 4) + step % 4, 4)
    return x * 4 + y


def choose(index, arrays):
    chosen = arrays[0]
    for i in range(1, len(arrays)):
        chosen = jnp.where(index == i, arrays[i], chosen)
    return chosen


CHIP_STEPS = [5, 4, 3, 7, 2, 6, 1]
COL_STEPS = [6, 2, 5, 7, 1, 3, 4]


def gather_kernel(
    groups_ref, panel_ref, b_ref, shift_ref, d_ref, t_ref,
    own, scat, panel, panel_t, pack, pack_in, strips, strip_cols, part, other, other_in, landed,
    scat_s, scat_r, ag_s, ag_r, dcore_s, dcore_r, drs_s, drs_r, dcol_s, dcol_r, dag_s, dag_r, dsib_s, dsib_r,
    core_s, core_r, rs_s, rs_r,
):
    grp, col, core, chip = where_am_i()
    sibling = {"grp": chip * 2 + (1 - core)}

    def at_chip(step):
        return {"grp": chip_peer(chip, step) * 2 + core}

    def at_col(step):
        return {"col": col_peer(col, step)}

    barrier = pltpu.get_barrier_semaphore()
    pl.semaphore_signal(barrier, 1, device_id=sibling, device_id_type=MESH)
    for step in range(1, CHIPS):
        pl.semaphore_signal(barrier, 1, device_id=at_chip(step), device_id_type=MESH)
    for step in range(1, COLS):
        pl.semaphore_signal(barrier, 1, device_id=at_col(step), device_id_type=MESH)

    sends = []

    def send(src, dst, s, r, to):
        copy = pltpu.make_async_remote_copy(
            src_ref=src, dst_ref=dst, send_sem=s, recv_sem=r, device_id=to, device_id_type=MESH
        )
        copy.start()
        sends.append(copy)
        return copy

    owner = panel_ref[0] // 4
    local = lax.rem(panel_ref[0], 4)
    live = groups_ref[grp]
    row = lax.broadcasted_iota(jnp.int32, (GROUP_ROWS, PANEL), 0)
    own[...] = jnp.where(row < live, choose(local, [b_ref[:, k * PANEL : (k + 1) * PANEL] for k in range(4)]), 0.0)

    pl.semaphore_wait(barrier, 15)

    mine_rows = pl.ds(pl.multiple_of(col * PIECE, PIECE), PIECE)
    scatters = []
    for i, step in enumerate(COL_STEPS):
        peer = col_peer(col, step)
        scatters.append(send(
            own.at[pl.ds(pl.multiple_of(peer * PIECE, PIECE), PIECE)], scat.at[col],
            scat_s.at[i], scat_r.at[i], at_col(step)))
    scat[col] = own[mine_rows, :]

    for k in range(4):
        pack[:, OFFSETS[k] : OFFSETS[k] + PANEL - k * B] = dot(
            own[:, k * B : (k + 1) * B], own[:, k * B :], ((0,), (0,)))
    half = pl.ds(pl.multiple_of(core * 64, 64), 64)
    half_other = pl.ds(pl.multiple_of((1 - core) * 64, 64), 64)
    swap = send(pack.at[half_other], pack_in, dcore_s, dcore_r, sibling)
    swap.wait_recv()
    pack[half, :] += pack_in[...]
    reduces = []
    for i, step in enumerate(CHIP_STEPS):
        peer = chip_peer(chip, step)
        reduces.append(send(
            pack.at[pl.ds(pl.multiple_of(core * 64 + peer * 8, 8), 8)], strips.at[i],
            drs_s.at[i], drs_r.at[i], at_chip(step)))

    for copy in scatters:
        copy.wait_recv()
    panel[mine_rows, :] = choose(owner, [scat[c] for c in range(COLS)])
    gathers = []
    for i, step in enumerate(COL_STEPS):
        gathers.append(send(panel.at[mine_rows], panel.at[mine_rows], ag_s.at[i], ag_r.at[i], at_col(step)))

    strip_at = pl.multiple_of(core * 64 + chip * 8, 8)
    strip_rows = pl.ds(strip_at, 8)
    total = pack[strip_rows, :]
    for i, copy in enumerate(reduces):
        copy.wait_recv()
        total += strips[i]
    lane = lax.broadcasted_iota(jnp.int32, (8, B), 1)
    sub = lax.broadcasted_iota(jnp.int32, (8, B), 0)
    for k in range(4):
        terms = choose(local, [shift_ref[:, p * PANEL + k * B : p * PANEL + (k + 1) * B] for p in range(4)])
        terms = jnp.broadcast_to(terms, (8, B))
        strip_cols[col, :, OFFSETS[k] : OFFSETS[k] + B] = total[:, OFFSETS[k] : OFFSETS[k] + B] + jnp.where(
            lane == strip_at + sub, terms, 0.0)
        if k < 3:
            strip_cols[col, :, OFFSETS[k] + B : OFFSETS[k + 1]] = total[:, OFFSETS[k] + B : OFFSETS[k + 1]]
    spreads = []
    for i, step in enumerate(COL_STEPS):
        spreads.append(send(strip_cols.at[col], strip_cols.at[col], dcol_s.at[i], dcol_r.at[i], at_col(step)))

    for copy in gathers:
        copy.wait_recv()
    panel_t[...] = panel[...].T

    for copy in spreads:
        copy.wait_recv()
    d_ref[strip_rows, :] = choose(owner, [strip_cols[c] for c in range(COLS)])
    dgathers = []
    for i, step in enumerate(CHIP_STEPS):
        dgathers.append(send(d_ref.at[strip_rows], d_ref.at[strip_rows], dag_s.at[i], dag_r.at[i], at_chip(step)))

    swaps, sums = {}, []
    steps = CHIP_STEPS + [0]

    def merge(i):
        swaps[i].wait_recv()
        part[i] += other_in[i]
        if steps[i]:
            sums.append(send(part.at[i], landed.at[i], rs_s.at[i], rs_r.at[i], at_chip(steps[i])))

    for i, step in enumerate(steps):
        peer = chip_peer(chip, step)
        both = dot(panel_t[...], b_ref[:, pl.ds(pl.multiple_of(peer * 2 * SHARE, 2 * SHARE), 2 * SHARE)])
        first, second = both[:, :SHARE], both[:, SHARE:]
        part[i] = jnp.where(core == 0, first, second)
        other[i] = jnp.where(core == 0, second, first)
        swaps[i] = send(other.at[i], other_in.at[i], core_s.at[i], core_r.at[i], sibling)
        if i >= 2:
            merge(i - 2)
    merge(len(steps) - 2)
    merge(len(steps) - 1)

    for copy in dgathers:
        copy.wait_recv()
    dswap = send(d_ref.at[half], d_ref.at[half], dsib_s, dsib_r, sibling)
    dswap.wait_recv()

    first_row = col * WIDTH + grp * SHARE - panel_ref[0] * PANEL
    terms = jnp.broadcast_to(
        shift_ref[:, pl.ds(pl.multiple_of(grp * SHARE, SHARE), SHARE)], (PANEL, SHARE))
    on_diag = first_row + lax.broadcasted_iota(jnp.int32, (PANEL, SHARE), 1) == lax.broadcasted_iota(
        jnp.int32, (PANEL, SHARE), 0)
    mine = part[len(steps) - 1] + jnp.where(on_diag, terms, 0.0)
    for i, copy in enumerate(sums):
        copy.wait_recv()
        mine += landed[i]
    t_ref[...] = mine
    for copy in sends:
        copy.wait_send()


def gathered(constraint_rows, shift, group_rows, panel_index):
    f32 = jnp.float32
    dma = pltpu.SemaphoreType.DMA
    vmem = pl.BlockSpec(memory_space=pltpu.VMEM)
    smem = pl.BlockSpec(memory_space=pltpu.SMEM)
    many = lambda n: [dma((n,)), dma((n,))]
    return pl.pallas_call(
        gather_kernel,
        out_shape=(jax.ShapeDtypeStruct((B, PACKED), f32), jax.ShapeDtypeStruct((PANEL, SHARE), f32)),
        in_specs=[smem, smem, vmem, vmem],
        out_specs=(vmem, vmem),
        scratch_shapes=[
            pltpu.VMEM((GROUP_ROWS, PANEL), f32),
            pltpu.VMEM((COLS, PIECE, PANEL), f32),
            pltpu.VMEM((GROUP_ROWS, PANEL), f32),
            pltpu.VMEM((PANEL, GROUP_ROWS), f32),
            pltpu.VMEM((B, PACKED), f32),
            pltpu.VMEM((64, PACKED), f32),
            pltpu.VMEM((7, 8, PACKED), f32),
            pltpu.VMEM((COLS, 8, PACKED), f32),
            pltpu.VMEM((8, PANEL, SHARE), f32),
            pltpu.VMEM((8, PANEL, SHARE), f32),
            pltpu.VMEM((8, PANEL, SHARE), f32),
            pltpu.VMEM((7, PANEL, SHARE), f32),
            *many(7), *many(7), dma, dma, *many(7), *many(7), *many(7), dma, dma, *many(8), *many(7),
        ],
        compiler_params=pltpu.CompilerParams(collective_id=0, has_side_effects=True, vmem_limit_bytes=40 << 20),
    )(group_rows, panel_index, constraint_rows, shift.reshape(1, -1))


def on_device(constraint_rows, shift, group_rows, panel_index):
    d, t = gathered(constraint_rows, shift, group_rows, panel_index)
    return solve(d, t)


def solution(mesh):
    placed = (P("grp", "col"), P("col"), P(), P())
    return jax.shard_map(
        on_device, mesh=mesh, in_specs=placed, out_specs=P(("col", "grp"), None), check_vma=False
    )
```

```python
import jax, jax.numpy as jnp
from jax import lax
from jax.experimental import pallas as pl
from jax.experimental.pallas import tpu as pltpu
from jax.sharding import PartitionSpec as P

B = 128
HI = lax.Precision.HIGHEST


def inv_chol(rows):
    lane = lax.broadcasted_iota(jnp.int32, (8, B), 1)
    rows = list(rows)
    for s in range(16):
        k0 = 8 * s
        inside = (lane >= k0) & (lane < k0 + 8)
        tile = rows[s]
        spread = lambda t, l: jnp.broadcast_to(t[:, k0 + l : k0 + l + 1], (8, B))
        cols = [spread(tile, l) for l in range(8)]
        c = {(m, l): jnp.broadcast_to(cols[l][m : m + 1, :], (8, B)) for l in range(8) for m in range(l, 8)}
        r = [
            jnp.where(inside, jnp.where(lane == k0 + m, 1.0, 0.0), jnp.broadcast_to(tile[m : m + 1, :], (8, B)))
            for m in range(8)
        ]
        rs, low = {}, {}
        for j in range(8):
            rs[j] = lax.rsqrt(c[j, j])
            r[j] = r[j] * rs[j]
            for m in range(j + 1, 8):
                low[m, j] = c[m, j] * rs[j]
            for m in range(j + 1, 8):
                for n in range(j + 1, m + 1):
                    c[m, n] = c[m, n] - low[m, j] * low[n, j]
                r[m] = r[m] - low[m, j] * r[j]
        sub = lax.broadcasted_iota(jnp.int32, (8, B), 0)
        done = r[0]
        for j in range(1, 8):
            done = jnp.where(sub == j, r[j], done)
        rows[s] = jnp.where(lane < k0 + 8, done, 0.0)
        if s < 15:
            g = list(r)
            for j in reversed(range(8)):
                for m in range(j + 1, 8):
                    g[j] = g[j] - low[m, j] * g[m]
                g[j] = g[j] * rs[j]
            for i in range(s + 1, 16):
                f = [spread(rows[i], l) for l in range(8)]
                t = jnp.where(inside, 0.0, rows[i])
                p0 = f[0] * g[0] + f[1] * g[1]
                p1 = f[2] * g[2] + f[3] * g[3]
                p2 = f[4] * g[4] + f[5] * g[5]
                p3 = f[6] * g[6] + f[7] * g[7]
                rows[i] = t - ((p0 + p1) + (p2 + p3))
    return rows


def dot(a, b, dims=((1,), (0,))):
    return lax.dot_general(a, b, (dims, ((), ())), precision=HI, preferred_element_type=jnp.float32)


GROUP_ROWS = 256
WIDTH = 2048
PANEL = 512
CHIPS = 8
COLS = 8
PIECE = GROUP_ROWS // COLS
SHARE = 128
OFFSETS = [0, 512, 896, 1152]
PACKED = 1280
MESH = pl.DeviceIdType.MESH


def where_am_i():
    grp, col = lax.axis_index("grp"), lax.axis_index("col")
    return grp, col, lax.rem(grp, 2), grp // 2


def chip_peer(chip, step):
    z = lax.rem(chip // 2 + step // 2, 4)
    x = lax.rem(lax.rem(chip, 2) + step % 2, 2)
    return z * 2 + x


def col_peer(col, step):
    x = lax.rem(col // 4 + step // 4, 2)
    y = lax.rem(lax.rem(col, 4) + step % 4, 4)
    return x * 4 + y


def choose(index, arrays):
    chosen = arrays[0]
    for i in range(1, len(arrays)):
        chosen = jnp.where(index == i, arrays[i], chosen)
    return chosen


CHIP_STEPS = [5, 4, 3, 7, 2, 6, 1]
COL_STEPS = [6, 2, 5, 7, 1, 3, 4]


def panel_kernel(
    groups_ref, panel_ref, b_ref, shift_ref, x_ref,
    d_ref, m_ref, t_ref, own, scat, panel, panel_t, pack, pack_in, strips, strip_cols, part, other, other_in, landed,
    scat_s, scat_r, ag_s, ag_r, dcore_s, dcore_r, drs_s, drs_r, dcol_s, dcol_r, dag_s, dag_r, dsib_s, dsib_r,
    core_s, core_r, rs_s, rs_r,
):
    grp, col, core, chip = where_am_i()
    sibling = {"grp": chip * 2 + (1 - core)}

    def at_chip(step):
        return {"grp": chip_peer(chip, step) * 2 + core}

    def at_col(step):
        return {"col": col_peer(col, step)}

    barrier = pltpu.get_barrier_semaphore()
    pl.semaphore_signal(barrier, 1, device_id=sibling, device_id_type=MESH)
    for step in range(1, CHIPS):
        pl.semaphore_signal(barrier, 1, device_id=at_chip(step), device_id_type=MESH)
    for step in range(1, COLS):
        pl.semaphore_signal(barrier, 1, device_id=at_col(step), device_id_type=MESH)

    sends = []

    def send(src, dst, s, r, to):
        copy = pltpu.make_async_remote_copy(
            src_ref=src, dst_ref=dst, send_sem=s, recv_sem=r, device_id=to, device_id_type=MESH
        )
        copy.start()
        sends.append(copy)
        return copy

    owner = panel_ref[0] // 4
    local = lax.rem(panel_ref[0], 4)
    live = groups_ref[grp]
    row = lax.broadcasted_iota(jnp.int32, (GROUP_ROWS, PANEL), 0)
    own[...] = jnp.where(row < live, choose(local, [b_ref[:, k * PANEL : (k + 1) * PANEL] for k in range(4)]), 0.0)

    pl.semaphore_wait(barrier, 15)

    mine_rows = pl.ds(pl.multiple_of(col * PIECE, PIECE), PIECE)
    scatters = []
    for i, step in enumerate(COL_STEPS):
        peer = col_peer(col, step)
        scatters.append(send(
            own.at[pl.ds(pl.multiple_of(peer * PIECE, PIECE), PIECE)], scat.at[col],
            scat_s.at[i], scat_r.at[i], at_col(step)))
    scat[col] = own[mine_rows, :]

    for k in range(4):
        pack[:, OFFSETS[k] : OFFSETS[k] + PANEL - k * B] = dot(
            own[:, k * B : (k + 1) * B], own[:, k * B :], ((0,), (0,)))
    half = pl.ds(pl.multiple_of(core * 64, 64), 64)
    half_other = pl.ds(pl.multiple_of((1 - core) * 64, 64), 64)
    swap = send(pack.at[half_other], pack_in, dcore_s, dcore_r, sibling)
    swap.wait_recv()
    pack[half, :] += pack_in[...]
    reduces = []
    for i, step in enumerate(CHIP_STEPS):
        peer = chip_peer(chip, step)
        reduces.append(send(
            pack.at[pl.ds(pl.multiple_of(core * 64 + peer * 8, 8), 8)], strips.at[i],
            drs_s.at[i], drs_r.at[i], at_chip(step)))

    for copy in scatters:
        copy.wait_recv()
    panel[mine_rows, :] = choose(owner, [scat[c] for c in range(COLS)])
    gathers = []
    for i, step in enumerate(COL_STEPS):
        gathers.append(send(panel.at[mine_rows], panel.at[mine_rows], ag_s.at[i], ag_r.at[i], at_col(step)))

    strip_at = pl.multiple_of(core * 64 + chip * 8, 8)
    strip_rows = pl.ds(strip_at, 8)
    total = pack[strip_rows, :]
    for i, copy in enumerate(reduces):
        copy.wait_recv()
        total += strips[i]
    lane = lax.broadcasted_iota(jnp.int32, (8, B), 1)
    sub = lax.broadcasted_iota(jnp.int32, (8, B), 0)
    for k in range(4):
        terms = choose(local, [shift_ref[:, p * PANEL + k * B : p * PANEL + (k + 1) * B] for p in range(4)])
        terms = jnp.broadcast_to(terms, (8, B))
        strip_cols[col, :, OFFSETS[k] : OFFSETS[k] + B] = total[:, OFFSETS[k] : OFFSETS[k] + B] + jnp.where(
            lane == strip_at + sub, terms, 0.0)
        if k < 3:
            strip_cols[col, :, OFFSETS[k] + B : OFFSETS[k + 1]] = total[:, OFFSETS[k] + B : OFFSETS[k + 1]]
    spreads = []
    for i, step in enumerate(COL_STEPS):
        spreads.append(send(strip_cols.at[col], strip_cols.at[col], dcol_s.at[i], dcol_r.at[i], at_col(step)))

    for copy in gathers:
        copy.wait_recv()
    panel_t[...] = panel[...].T

    for copy in spreads:
        copy.wait_recv()
    d_ref[strip_rows, :] = choose(owner, [strip_cols[c] for c in range(COLS)])
    dgathers = []
    for i, step in enumerate(CHIP_STEPS):
        dgathers.append(send(d_ref.at[strip_rows], d_ref.at[strip_rows], dag_s.at[i], dag_r.at[i], at_chip(step)))

    swaps, sums = {}, []
    steps = CHIP_STEPS + [0]

    def merge(i):
        swaps[i].wait_recv()
        part[i] += other_in[i]
        if steps[i]:
            sums.append(send(part.at[i], landed.at[i], rs_s.at[i], rs_r.at[i], at_chip(steps[i])))

    for i, step in enumerate(steps):
        peer = chip_peer(chip, step)
        both = dot(panel_t[...], b_ref[:, pl.ds(pl.multiple_of(peer * 2 * SHARE, 2 * SHARE), 2 * SHARE)])
        first, second = both[:, :SHARE], both[:, SHARE:]
        part[i] = jnp.where(core == 0, first, second)
        other[i] = jnp.where(core == 0, second, first)
        swaps[i] = send(other.at[i], other_in.at[i], core_s.at[i], core_r.at[i], sibling)
        if i >= 2:
            merge(i - 2)
    merge(len(steps) - 2)
    merge(len(steps) - 1)

    for copy in dgathers:
        copy.wait_recv()
    dswap = send(d_ref.at[half], d_ref.at[half], dsib_s, dsib_r, sibling)
    dswap.wait_recv()

    def sum_rows():
        first_row = col * WIDTH + grp * SHARE - panel_ref[0] * PANEL
        terms = jnp.broadcast_to(
            shift_ref[:, pl.ds(pl.multiple_of(grp * SHARE, SHARE), SHARE)], (PANEL, SHARE))
        on_diag = first_row + lax.broadcasted_iota(jnp.int32, (PANEL, SHARE), 1) == lax.broadcasted_iota(
            jnp.int32, (PANEL, SHARE), 0)
        mine = part[len(steps) - 1] + jnp.where(on_diag, terms, 0.0)
        for i, copy in enumerate(sums):
            copy.wait_recv()
            mine += landed[i]
        t_ref[...] = mine

    for k in range(4):
        m_ref[k * B : (k + 1) * B, k * B :] = d_ref[:, OFFSETS[k] : OFFSETS[k] + PANEL - k * B]
    inverses, uppers = [], []
    for k in range(4):
        if k == 3:
            sum_rows()
        at = k * B
        tiles = [m_ref[at + 8 * i : at + 8 * i + 8, at : at + B] for i in range(16)]
        w = jnp.concatenate(inv_chol(tiles), axis=0)
        inverses.append(w)
        if k == 3:
            break
        u = dot(w, m_ref[at : at + B, at + B :])
        uppers.append(u)
        for r in range(k + 1, 4):
            left = u[:, (r - k - 1) * B : (r - k) * B]
            m_ref[r * B : (r + 1) * B, r * B :] -= dot(left, u[:, (r - k - 1) * B :], ((0,), (0,)))
    rest = [t_ref[k * B : (k + 1) * B, :] for k in range(4)]
    for k in range(4):
        x = dot(inverses[k], rest[k])
        x_ref[:, k * B : (k + 1) * B] = x.T
        for r in range(k + 1, 4):
            rest[r] = rest[r] - dot(uppers[k][:, (r - k - 1) * B : (r - k) * B], x, ((0,), (0,)))
    for copy in sends:
        copy.wait_send()


def panel_rows(constraint_rows, shift, group_rows, panel_index):
    f32 = jnp.float32
    dma = pltpu.SemaphoreType.DMA
    vmem = pl.BlockSpec(memory_space=pltpu.VMEM)
    smem = pl.BlockSpec(memory_space=pltpu.SMEM)
    many = lambda n: [dma((n,)), dma((n,))]
    return pl.pallas_call(
        panel_kernel,
        out_shape=jax.ShapeDtypeStruct((SHARE, PANEL), f32),
        in_specs=[smem, smem, vmem, vmem],
        out_specs=vmem,
        scratch_shapes=[
            pltpu.VMEM((B, PACKED), f32),
            pltpu.VMEM((PANEL, PANEL), f32),
            pltpu.VMEM((PANEL, SHARE), f32),
            pltpu.VMEM((GROUP_ROWS, PANEL), f32),
            pltpu.VMEM((COLS, PIECE, PANEL), f32),
            pltpu.VMEM((GROUP_ROWS, PANEL), f32),
            pltpu.VMEM((PANEL, GROUP_ROWS), f32),
            pltpu.VMEM((B, PACKED), f32),
            pltpu.VMEM((64, PACKED), f32),
            pltpu.VMEM((7, 8, PACKED), f32),
            pltpu.VMEM((COLS, 8, PACKED), f32),
            pltpu.VMEM((8, PANEL, SHARE), f32),
            pltpu.VMEM((8, PANEL, SHARE), f32),
            pltpu.VMEM((8, PANEL, SHARE), f32),
            pltpu.VMEM((7, PANEL, SHARE), f32),
            *many(7), *many(7), dma, dma, *many(7), *many(7), *many(7), dma, dma, *many(8), *many(7),
        ],
        compiler_params=pltpu.CompilerParams(collective_id=0, has_side_effects=True, vmem_limit_bytes=40 << 20),
    )(group_rows, panel_index, constraint_rows, shift.reshape(1, -1))


def on_device(constraint_rows, shift, group_rows, panel_index):
    return panel_rows(constraint_rows, shift, group_rows, panel_index)


def solution(mesh):
    placed = (P("grp", "col"), P("col"), P(), P())
    return jax.shard_map(
        on_device, mesh=mesh, in_specs=placed, out_specs=P(("col", "grp"), None), check_vma=False
    )
```

```python
import jax, jax.numpy as jnp
from jax import lax
from jax.experimental import pallas as pl
from jax.experimental.pallas import tpu as pltpu
from jax.sharding import PartitionSpec as P

B = 128
HI = lax.Precision.HIGHEST


def inv_chol(rows):
    lane = lax.broadcasted_iota(jnp.int32, (8, B), 1)
    rows = list(rows)
    for s in range(16):
        k0 = 8 * s
        inside = (lane >= k0) & (lane < k0 + 8)
        tile = rows[s]
        spread = lambda t, l: jnp.broadcast_to(t[:, k0 + l : k0 + l + 1], (8, B))
        cols = [spread(tile, l) for l in range(8)]
        c = {(m, l): jnp.broadcast_to(cols[l][m : m + 1, :], (8, B)) for l in range(8) for m in range(l, 8)}
        r = [
            jnp.where(inside, jnp.where(lane == k0 + m, 1.0, 0.0), jnp.broadcast_to(tile[m : m + 1, :], (8, B)))
            for m in range(8)
        ]
        rs, low = {}, {}
        fs = [[spread(rows[i], l) for l in range(8)] for i in range(s + 1, min(s + 3, 16))]
        for j in range(8):
            rs[j] = lax.rsqrt(c[j, j])
            r[j] = r[j] * rs[j]
            for m in range(j + 1, 8):
                low[m, j] = c[m, j] * rs[j]
            for m in range(j + 1, 8):
                for n in range(j + 1, m + 1):
                    c[m, n] = c[m, n] - low[m, j] * low[n, j]
                r[m] = r[m] - low[m, j] * r[j]
        sub = lax.broadcasted_iota(jnp.int32, (8, B), 0)
        done = r[0]
        for j in range(1, 8):
            done = jnp.where(sub == j, r[j], done)
        rows[s] = jnp.where(lane < k0 + 8, done, 0.0)
        if s < 15:
            h = done.astype(jnp.bfloat16).astype(jnp.float32)
            mid = (done - h).astype(jnp.bfloat16).astype(jnp.float32)
            tail = done - h - mid
            lhs = jnp.concatenate([h, h, mid, h, tail, mid], axis=0).astype(jnp.bfloat16)
            rhs = jnp.concatenate([h, mid, h, tail, h, mid], axis=0).astype(jnp.bfloat16)
            late = lax.dot_general(lhs, rhs, (((0,), (0,)), ((), ())), preferred_element_type=jnp.float32)
            for i in range(s + 3, 16):
                rows[i] = jnp.where(inside, 0.0, rows[i]) - late[8 * i : 8 * i + 8, :]
            for d in range(2):
                if s + 1 + d < 16:
                    f = fs[d]
                    for j in range(8):
                        f[j] = f[j] * rs[j]
                        for m in range(j + 1, 8):
                            f[m] = f[m] - low[m, j] * f[j]
                    p0 = f[0] * r[0] + f[1] * r[1]
                    p1 = f[2] * r[2] + f[3] * r[3]
                    p2 = f[4] * r[4] + f[5] * r[5]
                    p3 = f[6] * r[6] + f[7] * r[7]
                    rows[s + 1 + d] = jnp.where(inside, 0.0, rows[s + 1 + d]) - ((p0 + p1) + (p2 + p3))
    return rows


def dot(a, b, dims=((1,), (0,))):
    return lax.dot_general(a, b, (dims, ((), ())), precision=HI, preferred_element_type=jnp.float32)


GROUP_ROWS = 256
WIDTH = 2048
PANEL = 512
CHIPS = 8
RING = 4
PIECE = GROUP_ROWS // RING
HALF = PANEL // 2
SHARE = 128
OFFSETS = [0, 512, 896, 1152]
PACKED = 1280
MESH = pl.DeviceIdType.MESH
AROUND = [2, 1, 3]
LAG = 4


def choose(index, arrays):
    chosen = arrays[0]
    for i in range(1, len(arrays)):
        chosen = jnp.where(index == i, arrays[i], chosen)
    return chosen


def panel_kernel(
    groups_hbm, panel_hbm, b_hbm, shift_hbm, x_ref,
    groups_ref, panel_ref, b_ref, shift_ref, d_ref, m_ref, own, scat, cross, panel, panel_t,
    pack, pack_in, strips, strip_y, strip_x, part, other, other_in, first_x, first_z, last_z, last_x,
    load_s, scat_s, scat_r, cross_s, cross_r, ag_s, ag_r, dcore_s, dcore_r, drs_s, drs_r, dy_s, dy_r, dx_s, dx_r,
    dag_s, dag_r, dsib_s, dsib_r, core_s, core_r, fx_s, fx_r, fz_s, fz_r, lz_s, lz_r, lx_s, lx_r,
):
    grp, col = lax.axis_index("grp"), lax.axis_index("col")
    z, x, core = grp // 4, lax.rem(grp // 2, 2), lax.rem(grp, 2)
    x_hi, y = col // RING, lax.rem(col, RING)

    def chip_of(dz, dx):
        return lax.rem(z + dz, RING) * 2 + lax.rem(x + dx, 2)

    def at_chip(dz, dx):
        return {"grp": chip_of(dz, dx) * 2 + core}

    def y_of(dy):
        return lax.rem(y + dy, RING)

    def at_y(dy):
        return {"col": x_hi * RING + y_of(dy)}

    sibling = {"grp": grp + 1 - 2 * core}
    across = {"col": (1 - x_hi) * RING + y}
    other_chips = [(dz, dx) for dx in (1, 0) for dz in AROUND + [0] if dz or dx]

    loads = [
        pltpu.make_async_copy(src, dst, load_s.at[i])
        for i, (src, dst) in enumerate(
            [(b_hbm, b_ref), (groups_hbm, groups_ref), (panel_hbm, panel_ref), (shift_hbm, shift_ref)])
    ]
    for copy in loads:
        copy.start()

    barrier = pltpu.get_barrier_semaphore()
    peers = [sibling, across] + [at_y(dy) for dy in AROUND] + [at_chip(*step) for step in other_chips]
    for peer in peers:
        pl.semaphore_signal(barrier, 1, device_id=peer, device_id_type=MESH)

    sends = []

    def send(src, dst, s, r, to):
        copy = pltpu.make_async_remote_copy(
            src_ref=src, dst_ref=dst, send_sem=s, recv_sem=r, device_id=to, device_id_type=MESH
        )
        copy.start()
        sends.append(copy)
        return copy

    def arrived(copies):
        for copy in copies:
            copy.wait_recv()

    for copy in loads[1:] + loads[:1]:
        copy.wait()
    owner = panel_ref[0] // 4
    owner_x, owner_y = owner // RING, lax.rem(owner, RING)
    local = lax.rem(panel_ref[0], 4)
    live = groups_ref[grp]
    row = lax.broadcasted_iota(jnp.int32, (GROUP_ROWS, PANEL), 0)
    own[...] = jnp.where(row < live, choose(local, [b_ref[:, k * PANEL : (k + 1) * PANEL] for k in range(4)]), 0.0)

    for k in range(4):
        pack[:, OFFSETS[k] : OFFSETS[k] + PANEL - k * B] = dot(
            own[:, k * B : (k + 1) * B], own[:, k * B :], ((0,), (0,)))
    pl.semaphore_wait(barrier, len(peers))

    half = pl.ds(pl.multiple_of(core * 64, 64), 64)
    half_other = pl.ds(pl.multiple_of((1 - core) * 64, 64), 64)
    swap = send(pack.at[half_other], pack_in, dcore_s, dcore_r, sibling)

    piece = pl.ds(pl.multiple_of(y * PIECE, PIECE), PIECE)
    columns = [pl.ds(h * HALF, HALF) for h in range(2)]
    scatters = [
        [
            send(own.at[pl.ds(pl.multiple_of(y_of(dy) * PIECE, PIECE), PIECE), columns[h]], scat.at[h, y],
                 scat_s.at[h, i], scat_r.at[h, i], at_y(dy))
            for i, dy in enumerate(AROUND)
        ]
        for h in range(2)
    ]
    for h in range(2):
        scat[h, y] = own[piece, h * HALF : (h + 1) * HALF]

    swap.wait_recv()
    pack[half, :] += pack_in[...]
    reduces = [
        send(pack.at[pl.ds(pl.multiple_of(core * 64 + chip_of(*step) * 8, 8), 8)], strips.at[i],
             drs_s.at[i], drs_r.at[i], at_chip(*step))
        for i, step in enumerate(other_chips)
    ]

    def pass_across(h):
        arrived(scatters[h])
        cross[h, x_hi] = choose(owner_y, [scat[h, i] for i in range(RING)])
        return send(cross.at[h, x_hi], cross.at[h, x_hi], cross_s.at[h], cross_r.at[h], across)

    def gather(h):
        crossings[h].wait_recv()
        panel[piece, h * HALF : (h + 1) * HALF] = choose(owner_x, [cross[h, i] for i in range(2)])
        return [
            send(panel.at[piece, columns[h]], panel.at[piece, columns[h]], ag_s.at[h, i], ag_r.at[h, i], at_y(dy))
            for i, dy in enumerate(AROUND)
        ]

    crossings = [pass_across(0)]

    strip_at = pl.multiple_of(core * 64 + (z * 2 + x) * 8, 8)
    strip_rows = pl.ds(strip_at, 8)
    total = pack[strip_rows, :]
    for i, copy in enumerate(reduces):
        copy.wait_recv()
        total += strips[i]
    lane = lax.broadcasted_iota(jnp.int32, (8, B), 1)
    sub = lax.broadcasted_iota(jnp.int32, (8, B), 0)
    for k in range(4):
        terms = choose(local, [shift_ref[:, p * PANEL + k * B : p * PANEL + (k + 1) * B] for p in range(4)])
        terms = jnp.broadcast_to(terms, (8, B))
        strip_y[y, :, OFFSETS[k] : OFFSETS[k] + B] = total[:, OFFSETS[k] : OFFSETS[k] + B] + jnp.where(
            lane == strip_at + sub, terms, 0.0)
        if k < 3:
            strip_y[y, :, OFFSETS[k] + B : OFFSETS[k + 1]] = total[:, OFFSETS[k] + B : OFFSETS[k + 1]]
    spreads = [
        send(strip_y.at[y], strip_y.at[y], dy_s.at[i], dy_r.at[i], at_y(dy)) for i, dy in enumerate(AROUND)
    ]

    crossings.append(pass_across(1))
    gathers = [gather(0)]
    gathers.append(gather(1))

    arrived(spreads)
    strip_x[x_hi] = choose(owner_y, [strip_y[i] for i in range(RING)])
    strip_cross = send(strip_x.at[x_hi], strip_x.at[x_hi], dx_s, dx_r, across)

    swaps, to_x, to_z = {}, {}, {}

    def gram(h, dz, dx):
        at = pl.multiple_of(chip_of(dz, dx) * 2 * SHARE, 2 * SHARE)
        both = dot(panel_t[h * HALF : (h + 1) * HALF, :], b_ref[:, pl.ds(at, 2 * SHARE)])
        first, second = both[:, :SHARE], both[:, SHARE:]
        part[h, dz, dx] = jnp.where(core == 0, first, second)
        other[h, dz, dx] = jnp.where(core == 0, second, first)
        swaps[h, dz, dx] = send(
            other.at[h, dz, dx], other_in.at[h, dz, dx], core_s.at[h, dz, dx], core_r.at[h, dz, dx], sibling)

    def merge(h, dz, dx):
        swaps[h, dz, dx].wait_recv()
        part[h, dz, dx] += other_in[h, dz, dx]
        if h == 0 and dx == 1:
            to_x[dz] = send(part.at[0, dz, 1], first_x.at[dz], fx_s.at[dz], fx_r.at[dz], at_chip(0, 1))
        if h == 1 and dx == 0 and dz:
            to_z[dz] = send(part.at[1, dz], last_z.at[dz], lz_s.at[dz], lz_r.at[dz], at_chip(dz, 0))

    def pass_on_z(dz):
        to_x[dz].wait_recv()
        part[0, dz, 0] += first_x[dz]
        if dz:
            from_z.append(send(part.at[0, dz, 0], first_z.at[dz], fz_s.at[dz], fz_r.at[dz], at_chip(dz, 0)))

    def pass_on_x():
        for dz in AROUND:
            to_z[dz].wait_recv()
            part[1, 0] += last_z[dz]
        return send(part.at[1, 0, 1], last_x, lx_s, lx_r, at_chip(0, 1))

    from_z = []
    order = [(h, dz, dx) for h in range(2) for dz, dx in (
        [(dz, dx) for dx in (1, 0) for dz in AROUND + [0]] if h == 0
        else [(dz, dx) for dz in AROUND + [0] for dx in (1, 0)])]
    for i, step in enumerate(order):
        h = step[0]
        if i == 8 * h:
            arrived(gathers[h])
            panel_t[h * HALF : (h + 1) * HALF, :] = panel[:, h * HALF : (h + 1) * HALF].T
        gram(*step)
        if i == LAG:
            strip_cross.wait_recv()
            d_ref[strip_rows, :] = choose(owner_x, [strip_x[c] for c in range(2)])
            dgathers = [
                send(d_ref.at[strip_rows], d_ref.at[strip_rows], dag_s.at[c], dag_r.at[c], at_chip(*chip))
                for c, chip in enumerate(other_chips)
            ]
        if i >= LAG:
            merge(*order[i - LAG])
    for step in order[-LAG:]:
        merge(*step)
    arrived(dgathers)
    dswap = send(d_ref.at[half], d_ref.at[half], dsib_s, dsib_r, sibling)
    pass_on_z(2)
    dswap.wait_recv()

    first_row = col * WIDTH + grp * SHARE - panel_ref[0] * PANEL
    terms = jnp.broadcast_to(shift_ref[:, pl.ds(pl.multiple_of(grp * SHARE, SHARE), SHARE)], (HALF, SHARE))

    def rows(h, total):
        at_row = h * HALF + lax.broadcasted_iota(jnp.int32, (HALF, SHARE), 0)
        on_diag = first_row + lax.broadcasted_iota(jnp.int32, (HALF, SHARE), 1) == at_row
        total = part[h, 0, 0] + jnp.where(on_diag, terms, 0.0) + total
        return [total[:B, :], total[B:, :]]

    def solved(k, right):
        x_k = dot(inverses[k], right)
        x_ref[:, k * B : (k + 1) * B] = x_k.T
        return x_k

    def under(k, left, right):
        return dot(uppers[k][:, left * B : right * B], x_rows[k], ((0,), (0,)))

    for k in range(4):
        m_ref[k * B : (k + 1) * B, k * B :] = d_ref[:, OFFSETS[k] : OFFSETS[k] + PANEL - k * B]
    inverses, uppers = [], []
    for k in range(4):
        if k == 1:
            pass_on_z(1)
            pass_on_z(3)
        if k == 2:
            pass_on_z(0)
            from_x = pass_on_x()
        if k == 3:
            arrived(from_z)
            upper_rows = rows(0, first_z[1] + first_z[2] + first_z[3])
            x_rows = [solved(0, upper_rows[0])]
            x_rows.append(solved(1, upper_rows[1] - under(0, 0, 1)))
            carried = under(0, 1, 3) + under(1, 0, 2)
        at = k * B
        tiles = [m_ref[at + 8 * i : at + 8 * i + 8, at : at + B] for i in range(16)]
        w = jnp.concatenate(inv_chol(tiles), axis=0)
        inverses.append(w)
        if k == 3:
            break
        u = dot(w, m_ref[at : at + B, at + B :])
        uppers.append(u)
        for r in range(k + 1, 4):
            left = u[:, (r - k - 1) * B : (r - k) * B]
            m_ref[r * B : (r + 1) * B, r * B :] -= dot(left, u[:, (r - k - 1) * B :], ((0,), (0,)))
    from_x.wait_recv()
    lower_rows = rows(1, last_x[...])
    x_rows.append(solved(2, lower_rows[0] - carried[:B, :]))
    solved(3, lower_rows[1] - carried[B:, :] - under(2, 0, 1))
    for copy in sends:
        copy.wait_send()


def panel_rows(constraint_rows, shift, group_rows, panel_index):
    f32 = jnp.float32
    dma = pltpu.SemaphoreType.DMA
    buf = lambda *shape: pltpu.VMEM(shape, f32)
    pair = lambda *shape: [dma(*shape) if shape else dma] * 2
    return pl.pallas_call(
        panel_kernel,
        out_shape=jax.ShapeDtypeStruct((SHARE, PANEL), f32),
        in_specs=[pl.BlockSpec(memory_space=pl.ANY)] * 4,
        out_specs=pl.BlockSpec(memory_space=pltpu.VMEM),
        scratch_shapes=[
            pltpu.SMEM((16,), jnp.int32),
            pltpu.SMEM((1,), jnp.int32),
            buf(GROUP_ROWS, WIDTH),
            buf(1, WIDTH),
            buf(B, PACKED),
            buf(PANEL, PANEL),
            buf(GROUP_ROWS, PANEL),
            buf(2, RING, PIECE, HALF),
            buf(2, 2, PIECE, HALF),
            buf(GROUP_ROWS, PANEL),
            buf(PANEL, GROUP_ROWS),
            buf(B, PACKED),
            buf(64, PACKED),
            buf(7, 8, PACKED),
            buf(RING, 8, PACKED),
            buf(2, 8, PACKED),
            *[buf(2, RING, 2, HALF, SHARE)] * 3,
            buf(RING, HALF, SHARE),
            buf(RING, HALF, SHARE),
            buf(RING, 2, HALF, SHARE),
            buf(HALF, SHARE),
            dma((4,)),
            *pair((2, 3)), *pair((2,)), *pair((2, 3)), *pair(), *pair((7,)), *pair((3,)), *pair(),
            *pair((7,)), *pair(), *pair((2, RING, 2)), *pair((RING,)), *pair((RING,)), *pair((RING,)), *pair(),
        ],
        compiler_params=pltpu.CompilerParams(collective_id=0, has_side_effects=True, vmem_limit_bytes=56 << 20),
    )(group_rows, panel_index, constraint_rows, shift.reshape(1, -1))


def on_device(constraint_rows, shift, group_rows, panel_index):
    return panel_rows(constraint_rows, shift, group_rows, panel_index)


def solution(mesh):
    placed = (P("grp", "col"), P("col"), P(), P())
    return jax.shard_map(
        on_device, mesh=mesh, in_specs=placed, out_specs=P(("col", "grp"), None), check_vma=False
    )
```

```python
import jax, jax.numpy as jnp
from jax import lax
from jax.experimental import pallas as pl
from jax.experimental.pallas import tpu as pltpu
from jax.sharding import PartitionSpec as P

B = 128
HI = lax.Precision.HIGHEST


def inv_chol(rows, midway=None):
    lane = lax.broadcasted_iota(jnp.int32, (8, B), 1)
    rows = list(rows)
    for s in range(16):
        k0 = 8 * s
        if s == 8 and midway:
            midway()
        inside = (lane >= k0) & (lane < k0 + 8)
        tile = rows[s]
        spread = lambda t, l: jnp.broadcast_to(t[:, k0 + l : k0 + l + 1], (8, B))
        cols = [spread(tile, l) for l in range(8)]
        c = {(m, l): jnp.broadcast_to(cols[l][m : m + 1, :], (8, B)) for l in range(8) for m in range(l, 8)}
        r = [
            jnp.where(inside, jnp.where(lane == k0 + m, 1.0, 0.0), jnp.broadcast_to(tile[m : m + 1, :], (8, B)))
            for m in range(8)
        ]
        rs, low = {}, {}
        fs = [[spread(rows[i], l) for l in range(8)] for i in range(s + 1, min(s + 3, 16))]
        for j in range(8):
            rs[j] = lax.rsqrt(c[j, j])
            r[j] = r[j] * rs[j]
            for m in range(j + 1, 8):
                low[m, j] = c[m, j] * rs[j]
            for m in range(j + 1, 8):
                for n in range(j + 1, m + 1):
                    c[m, n] = c[m, n] - low[m, j] * low[n, j]
                r[m] = r[m] - low[m, j] * r[j]
        sub = lax.broadcasted_iota(jnp.int32, (8, B), 0)
        done = r[0]
        for j in range(1, 8):
            done = jnp.where(sub == j, r[j], done)
        rows[s] = jnp.where(lane < k0 + 8, done, 0.0)
        if s < 15:
            h = done.astype(jnp.bfloat16).astype(jnp.float32)
            mid = (done - h).astype(jnp.bfloat16).astype(jnp.float32)
            tail = done - h - mid
            lhs = jnp.concatenate([h, h, mid, h, tail, mid], axis=0).astype(jnp.bfloat16)
            rhs = jnp.concatenate([h, mid, h, tail, h, mid], axis=0).astype(jnp.bfloat16)
            late = lax.dot_general(lhs, rhs, (((0,), (0,)), ((), ())), preferred_element_type=jnp.float32)
            for i in range(s + 3, 16):
                rows[i] = jnp.where(inside, 0.0, rows[i]) - late[8 * i : 8 * i + 8, :]
            for d in range(2):
                if s + 1 + d < 16:
                    f = fs[d]
                    for j in range(8):
                        f[j] = f[j] * rs[j]
                        for m in range(j + 1, 8):
                            f[m] = f[m] - low[m, j] * f[j]
                    p0 = f[0] * r[0] + f[1] * r[1]
                    p1 = f[2] * r[2] + f[3] * r[3]
                    p2 = f[4] * r[4] + f[5] * r[5]
                    p3 = f[6] * r[6] + f[7] * r[7]
                    rows[s + 1 + d] = jnp.where(inside, 0.0, rows[s + 1 + d]) - ((p0 + p1) + (p2 + p3))
    return rows


def dot(a, b, dims=((1,), (0,))):
    return lax.dot_general(a, b, (dims, ((), ())), precision=HI, preferred_element_type=jnp.float32)


GROUP_ROWS = 256
WIDTH = 2048
PANEL = 512
CHIPS = 8
RING = 4
PIECE = GROUP_ROWS // RING
HALF = PANEL // 2
SHARE = 128
OFFSETS = [0, 512, 896, 1152]
PACKED = 1280
MESH = pl.DeviceIdType.MESH
AROUND = [2, 1, 3]
LAG = 2


def choose(index, arrays):
    chosen = arrays[0]
    for i in range(1, len(arrays)):
        chosen = jnp.where(index == i, arrays[i], chosen)
    return chosen


def panel_kernel(
    groups_hbm, panel_hbm, b_hbm, shift_hbm, x_ref,
    groups_ref, panel_ref, b_ref, shift_ref, d_ref, m_ref, own, scat, cross, panel, panel_t,
    pack, pack_in, strips, strip_y, strip_x, part, other, other_in, first_x, first_z, last_z, last_x,
    load_s, scat_s, scat_r, cross_s, cross_r, ag_s, ag_r, dcore_s, dcore_r, drs_s, drs_r, dy_s, dy_r, dx_s, dx_r,
    dag_s, dag_r, dsib_s, dsib_r, core_s, core_r, fx_s, fx_r, fz_s, fz_r, lz_s, lz_r, lx_s, lx_r,
):
    grp, col = lax.axis_index("grp"), lax.axis_index("col")
    z, x, core = grp // 4, lax.rem(grp // 2, 2), lax.rem(grp, 2)
    x_hi, y = col // RING, lax.rem(col, RING)

    def chip_of(dz, dx):
        return lax.rem(z + dz, RING) * 2 + lax.rem(x + dx, 2)

    def at_chip(dz, dx):
        return {"grp": chip_of(dz, dx) * 2 + core}

    def y_of(dy):
        return lax.rem(y + dy, RING)

    def at_y(dy):
        return {"col": x_hi * RING + y_of(dy)}

    sibling = {"grp": grp + 1 - 2 * core}
    across = {"col": (1 - x_hi) * RING + y}
    other_chips = [(dz, dx) for dx in (1, 0) for dz in AROUND + [0] if dz or dx]

    loads = [
        pltpu.make_async_copy(src, dst, load_s.at[i])
        for i, (src, dst) in enumerate(
            [(b_hbm, b_ref), (groups_hbm, groups_ref), (panel_hbm, panel_ref), (shift_hbm, shift_ref)])
    ]
    for copy in loads:
        copy.start()

    barrier = pltpu.get_barrier_semaphore()
    peers = [sibling, across] + [at_y(dy) for dy in AROUND] + [at_chip(*step) for step in other_chips]
    for peer in peers:
        pl.semaphore_signal(barrier, 1, device_id=peer, device_id_type=MESH)

    sends = []

    def send(src, dst, s, r, to):
        copy = pltpu.make_async_remote_copy(
            src_ref=src, dst_ref=dst, send_sem=s, recv_sem=r, device_id=to, device_id_type=MESH
        )
        copy.start()
        sends.append(copy)
        return copy

    def arrived(copies):
        for copy in copies:
            copy.wait_recv()

    for copy in loads[1:] + loads[:1]:
        copy.wait()
    owner = panel_ref[0] // 4
    owner_x, owner_y = owner // RING, lax.rem(owner, RING)
    local = lax.rem(panel_ref[0], 4)
    live = groups_ref[grp]
    row = lax.broadcasted_iota(jnp.int32, (GROUP_ROWS, PANEL), 0)
    own[...] = jnp.where(row < live, choose(local, [b_ref[:, k * PANEL : (k + 1) * PANEL] for k in range(4)]), 0.0)

    for k in range(4):
        pack[:, OFFSETS[k] : OFFSETS[k] + PANEL - k * B] = dot(
            own[:, k * B : (k + 1) * B], own[:, k * B :], ((0,), (0,)))
    pl.semaphore_wait(barrier, len(peers))

    half = pl.ds(pl.multiple_of(core * 64, 64), 64)
    half_other = pl.ds(pl.multiple_of((1 - core) * 64, 64), 64)
    swap = send(pack.at[half_other], pack_in, dcore_s, dcore_r, sibling)

    piece = pl.ds(pl.multiple_of(y * PIECE, PIECE), PIECE)
    columns = [pl.ds(h * HALF, HALF) for h in range(2)]
    scatters = [
        [
            send(own.at[pl.ds(pl.multiple_of(y_of(dy) * PIECE, PIECE), PIECE), columns[h]], scat.at[h, y],
                 scat_s.at[h, i], scat_r.at[h, i], at_y(dy))
            for i, dy in enumerate(AROUND)
        ]
        for h in range(2)
    ]
    for h in range(2):
        scat[h, y] = own[piece, h * HALF : (h + 1) * HALF]

    swap.wait_recv()
    pack[half, :] += pack_in[...]
    reduces = [
        send(pack.at[pl.ds(pl.multiple_of(core * 64 + chip_of(*step) * 8, 8), 8)], strips.at[i],
             drs_s.at[i], drs_r.at[i], at_chip(*step))
        for i, step in enumerate(other_chips)
    ]

    def pass_across(h):
        arrived(scatters[h])
        cross[h, x_hi] = choose(owner_y, [scat[h, i] for i in range(RING)])
        return send(cross.at[h, x_hi], cross.at[h, x_hi], cross_s.at[h], cross_r.at[h], across)

    def gather(h):
        crossings[h].wait_recv()
        panel[piece, h * HALF : (h + 1) * HALF] = choose(owner_x, [cross[h, i] for i in range(2)])
        return [
            send(panel.at[piece, columns[h]], panel.at[piece, columns[h]], ag_s.at[h, i], ag_r.at[h, i], at_y(dy))
            for i, dy in enumerate(AROUND)
        ]

    crossings = [pass_across(0)]

    strip_at = pl.multiple_of(core * 64 + (z * 2 + x) * 8, 8)
    strip_rows = pl.ds(strip_at, 8)
    total = pack[strip_rows, :]
    for i, copy in enumerate(reduces):
        copy.wait_recv()
        total += strips[i]
    lane = lax.broadcasted_iota(jnp.int32, (8, B), 1)
    sub = lax.broadcasted_iota(jnp.int32, (8, B), 0)
    for k in range(4):
        terms = choose(local, [shift_ref[:, p * PANEL + k * B : p * PANEL + (k + 1) * B] for p in range(4)])
        terms = jnp.broadcast_to(terms, (8, B))
        strip_y[y, :, OFFSETS[k] : OFFSETS[k] + B] = total[:, OFFSETS[k] : OFFSETS[k] + B] + jnp.where(
            lane == strip_at + sub, terms, 0.0)
        if k < 3:
            strip_y[y, :, OFFSETS[k] + B : OFFSETS[k + 1]] = total[:, OFFSETS[k] + B : OFFSETS[k + 1]]
    spreads = [
        send(strip_y.at[y], strip_y.at[y], dy_s.at[i], dy_r.at[i], at_y(dy)) for i, dy in enumerate(AROUND)
    ]

    crossings.append(pass_across(1))
    gathers = [gather(0)]
    gathers.append(gather(1))

    arrived(spreads)
    strip_x[x_hi] = choose(owner_y, [strip_y[i] for i in range(RING)])
    strip_cross = send(strip_x.at[x_hi], strip_x.at[x_hi], dx_s, dx_r, across)

    strip_cross.wait_recv()
    d_ref[strip_rows, :] = choose(owner_x, [strip_x[c] for c in range(2)])
    parts = [pl.ds(0, B), pl.ds(B, PACKED - B)]
    dgathers = [
        [
            send(d_ref.at[strip_rows, cols], d_ref.at[strip_rows, cols], dag_s.at[p, c], dag_r.at[p, c], at_chip(*chip))
            for c, chip in enumerate(other_chips)
        ]
        for p, cols in enumerate(parts)
    ]

    def to_sibling(p):
        arrived(dgathers[p])
        return send(d_ref.at[half, parts[p]], d_ref.at[half, parts[p]], dsib_s.at[p], dsib_r.at[p], sibling)


    swaps, to_x, to_z = {}, {}, {}

    def gram(h, dz):
        at = pl.multiple_of(lax.rem(z + dz, RING) * 4 * SHARE, 4 * SHARE)
        block = dot(panel_t[h * HALF : (h + 1) * HALF, :], b_ref[:, pl.ds(at, 4 * SHARE)])
        for chip_x in range(2):
            dx = lax.rem(x + chip_x, 2)
            first, second = (block[:, (2 * chip_x + c) * SHARE : (2 * chip_x + c + 1) * SHARE] for c in range(2))
            part[h, dz, dx] = jnp.where(core == 0, first, second)
            other[h, dz, dx] = jnp.where(core == 0, second, first)
        swaps[h, dz] = send(other.at[h, dz], other_in.at[h, dz], core_s.at[h, dz], core_r.at[h, dz], sibling)

    def merge(h, dz):
        swaps[h, dz].wait_recv()
        part[h, dz] += other_in[h, dz]
        if h == 1:
            to_x[dz] = send(part.at[1, dz, 1], first_x.at[dz], fx_s.at[dz], fx_r.at[dz], at_chip(0, 1))
        elif dz:
            to_z[dz] = send(part.at[0, dz], last_z.at[dz], lz_s.at[dz], lz_r.at[dz], at_chip(dz, 0))

    def pass_on_z(dz):
        to_x[dz].wait_recv()
        part[1, dz, 0] += first_x[dz]
        if dz:
            from_z.append(send(part.at[1, dz, 0], first_z.at[dz], fz_s.at[dz], fz_r.at[dz], at_chip(dz, 0)))

    def pass_on_x():
        for dz in AROUND:
            to_z[dz].wait_recv()
            part[0, 0] += last_z[dz]
        return send(part.at[0, 0, 1], last_x, lx_s, lx_r, at_chip(0, 1))

    from_z = []
    order = [(h, dz) for h in range(2) for dz in AROUND + [0]]
    for i, (h, dz) in enumerate(order):
        if i == 4 * h:
            arrived(gathers[h])
            panel_t[h * HALF : (h + 1) * HALF, :] = panel[:, h * HALF : (h + 1) * HALF].T
        gram(h, dz)
        if i >= LAG:
            merge(*order[i - LAG])
    for step in order[-LAG:]:
        merge(*step)
    to_sibling(0).wait_recv()

    first_row = col * WIDTH + grp * SHARE - panel_ref[0] * PANEL
    terms = jnp.broadcast_to(shift_ref[:, pl.ds(pl.multiple_of(grp * SHARE, SHARE), SHARE)], (HALF, SHARE))

    def rows(h, total):
        at_row = h * HALF + lax.broadcasted_iota(jnp.int32, (HALF, SHARE), 0)
        on_diag = first_row + lax.broadcasted_iota(jnp.int32, (HALF, SHARE), 1) == at_row
        total = part[h, 0, 0] + jnp.where(on_diag, terms, 0.0) + total
        return [total[:B, :], total[B:, :]]

    def solved(k, right):
        x_k = dot(inverses[k], right)
        x_ref[:, k * B : (k + 1) * B] = x_k.T
        return x_k

    def under(k, left, right):
        return dot(uppers[k][:, left * B : right * B], x_rows[k], ((0,), (0,)))

    inverses, uppers = [], []
    summed_z = []
    between = {1: lambda: (summed_z.append(pass_on_x()), pass_on_z(3)), 2: lambda: pass_on_z(0)}
    for k in range(4):
        if k == 1:
            pass_on_z(2)
            pass_on_z(1)
        if k == 3:
            summed_z[0].wait_recv()
            upper_rows = rows(0, last_x[...])
            x_rows = [solved(0, upper_rows[0])]
            x_rows.append(solved(1, upper_rows[1] - under(0, 0, 1)))
            carried = under(0, 1, 3) + under(1, 0, 2)
        at = k * B
        if k == 0:
            rest = []
            tiles = [d_ref[8 * i : 8 * i + 8, :B] for i in range(16)]
            tiles = inv_chol(tiles, lambda: rest.append(to_sibling(1)))
            rest[0].wait_recv()
            for r in range(4):
                m_ref[r * B : (r + 1) * B, r * B :] = d_ref[:, OFFSETS[r] : OFFSETS[r] + PANEL - r * B]
        else:
            tiles = inv_chol([m_ref[at + 8 * i : at + 8 * i + 8, at : at + B] for i in range(16)], between.get(k))
        w = jnp.concatenate(tiles, axis=0)
        inverses.append(w)
        if k == 3:
            break
        u = dot(w, m_ref[at : at + B, at + B :])
        uppers.append(u)
        for r in range(k + 1, 4):
            left = u[:, (r - k - 1) * B : (r - k) * B]
            m_ref[r * B : (r + 1) * B, r * B :] -= dot(left, u[:, (r - k - 1) * B :], ((0,), (0,)))
    arrived(from_z)
    lower_rows = rows(1, first_z[1] + first_z[2] + first_z[3])
    x_rows.append(solved(2, lower_rows[0] - carried[:B, :]))
    solved(3, lower_rows[1] - carried[B:, :] - under(2, 0, 1))
    for copy in sends:
        copy.wait_send()


def panel_rows(constraint_rows, shift, group_rows, panel_index):
    f32 = jnp.float32
    dma = pltpu.SemaphoreType.DMA
    buf = lambda *shape: pltpu.VMEM(shape, f32)
    pair = lambda *shape: [dma(*shape) if shape else dma] * 2
    return pl.pallas_call(
        panel_kernel,
        out_shape=jax.ShapeDtypeStruct((SHARE, PANEL), f32),
        in_specs=[pl.BlockSpec(memory_space=pl.ANY)] * 4,
        out_specs=pl.BlockSpec(memory_space=pltpu.VMEM),
        scratch_shapes=[
            pltpu.SMEM((16,), jnp.int32),
            pltpu.SMEM((1,), jnp.int32),
            buf(GROUP_ROWS, WIDTH),
            buf(1, WIDTH),
            buf(B, PACKED),
            buf(PANEL, PANEL),
            buf(GROUP_ROWS, PANEL),
            buf(2, RING, PIECE, HALF),
            buf(2, 2, PIECE, HALF),
            buf(GROUP_ROWS, PANEL),
            buf(PANEL, GROUP_ROWS),
            buf(B, PACKED),
            buf(64, PACKED),
            buf(7, 8, PACKED),
            buf(RING, 8, PACKED),
            buf(2, 8, PACKED),
            *[buf(2, RING, 2, HALF, SHARE)] * 3,
            buf(RING, HALF, SHARE),
            buf(RING, HALF, SHARE),
            buf(RING, 2, HALF, SHARE),
            buf(HALF, SHARE),
            dma((4,)),
            *pair((2, 3)), *pair((2,)), *pair((2, 3)), *pair(), *pair((7,)), *pair((3,)), *pair(),
            *pair((2, 7)), *pair((2,)), *pair((2, RING)), *pair((RING,)), *pair((RING,)), *pair((RING,)), *pair(),
        ],
        compiler_params=pltpu.CompilerParams(collective_id=0, has_side_effects=True, vmem_limit_bytes=56 << 20),
    )(group_rows, panel_index, constraint_rows, shift.reshape(1, -1))


def on_device(constraint_rows, shift, group_rows, panel_index):
    return panel_rows(constraint_rows, shift, group_rows, panel_index)


def solution(mesh):
    placed = (P("grp", "col"), P("col"), P(), P())
    return jax.shard_map(
        on_device, mesh=mesh, in_specs=placed, out_specs=P(("col", "grp"), None), check_vma=False
    )
```

```python
import jax, jax.numpy as jnp
from jax import lax
from jax.experimental import pallas as pl
from jax.experimental.pallas import tpu as pltpu
from jax.sharding import PartitionSpec as P

B = 128
HI = lax.Precision.HIGHEST


def inv_chol(rows, midway=None):
    lane = lax.broadcasted_iota(jnp.int32, (8, B), 1)
    rows = list(rows)
    for s in range(16):
        k0 = 8 * s
        if s == 8 and midway:
            midway()
        inside = (lane >= k0) & (lane < k0 + 8)
        tile = rows[s]
        spread = lambda t, l: jnp.broadcast_to(t[:, k0 + l : k0 + l + 1], (8, B))
        cols = [spread(tile, l) for l in range(8)]
        c = {(m, l): jnp.broadcast_to(cols[l][m : m + 1, :], (8, B)) for l in range(8) for m in range(l, 8)}
        r = [
            jnp.where(inside, jnp.where(lane == k0 + m, 1.0, 0.0), jnp.broadcast_to(tile[m : m + 1, :], (8, B)))
            for m in range(8)
        ]
        rs, low = {}, {}
        fs = [[spread(rows[i], l) for l in range(8)] for i in range(s + 1, min(s + 3, 16))]
        for j in range(8):
            rs[j] = lax.rsqrt(c[j, j])
            r[j] = r[j] * rs[j]
            for m in range(j + 1, 8):
                low[m, j] = c[m, j] * rs[j]
            for m in range(j + 1, 8):
                for n in range(j + 1, m + 1):
                    c[m, n] = c[m, n] - low[m, j] * low[n, j]
                r[m] = r[m] - low[m, j] * r[j]
        sub = lax.broadcasted_iota(jnp.int32, (8, B), 0)
        done = r[0]
        for j in range(1, 8):
            done = jnp.where(sub == j, r[j], done)
        rows[s] = jnp.where(lane < k0 + 8, done, 0.0)
        if s < 15:
            h = done.astype(jnp.bfloat16).astype(jnp.float32)
            mid = (done - h).astype(jnp.bfloat16).astype(jnp.float32)
            tail = done - h - mid
            lhs = jnp.concatenate([h, h, mid, h, tail, mid], axis=0).astype(jnp.bfloat16)
            rhs = jnp.concatenate([h, mid, h, tail, h, mid], axis=0).astype(jnp.bfloat16)
            late = lax.dot_general(lhs, rhs, (((0,), (0,)), ((), ())), preferred_element_type=jnp.float32)
            for i in range(s + 3, 16):
                rows[i] = jnp.where(inside, 0.0, rows[i]) - late[8 * i : 8 * i + 8, :]
            for d in range(2):
                if s + 1 + d < 16:
                    f = fs[d]
                    for j in range(8):
                        f[j] = f[j] * rs[j]
                        for m in range(j + 1, 8):
                            f[m] = f[m] - low[m, j] * f[j]
                    p0 = f[0] * r[0] + f[1] * r[1]
                    p1 = f[2] * r[2] + f[3] * r[3]
                    p2 = f[4] * r[4] + f[5] * r[5]
                    p3 = f[6] * r[6] + f[7] * r[7]
                    rows[s + 1 + d] = jnp.where(inside, 0.0, rows[s + 1 + d]) - ((p0 + p1) + (p2 + p3))
    return rows


def dot(a, b, dims=((1,), (0,))):
    return lax.dot_general(a, b, (dims, ((), ())), precision=HI, preferred_element_type=jnp.float32)


GROUP_ROWS = 256
WIDTH = 2048
PANEL = 512
CHIPS = 8
RING = 4
PIECE = GROUP_ROWS // RING
HALF = PANEL // 2
SHARE = 128
OFFSETS = [0, 512, 896, 1152]
PACKED = 1280
MESH = pl.DeviceIdType.MESH
AROUND = [2, 1, 3]
LAG = 2


def choose(index, arrays):
    chosen = arrays[0]
    for i in range(1, len(arrays)):
        chosen = jnp.where(index == i, arrays[i], chosen)
    return chosen


def panel_kernel(
    groups_hbm, panel_hbm, b_hbm, shift_hbm, x_ref,
    groups_ref, panel_ref, b_ref, shift_ref, d_ref, m_ref, own, scat, cross, panel, panel_t,
    pack, pack_in, strips, strip_y, strip_x, part, other, other_in, first_x, first_z, last_z, last_x,
    load_s, scat_s, scat_r, cross_s, cross_r, ag_s, ag_r, dcore_s, dcore_r, drs_s, drs_r, dy_s, dy_r, dx_s, dx_r,
    dag_s, dag_r, dsib_s, dsib_r, core_s, core_r, fx_s, fx_r, fz_s, fz_r, lz_s, lz_r, lx_s, lx_r,
):
    grp, col = lax.axis_index("grp"), lax.axis_index("col")
    z, x, core = grp // 4, lax.rem(grp // 2, 2), lax.rem(grp, 2)
    x_hi, y = col // RING, lax.rem(col, RING)

    def chip_of(dz, dx):
        return lax.rem(z + dz, RING) * 2 + lax.rem(x + dx, 2)

    def at_chip(dz, dx):
        return {"grp": chip_of(dz, dx) * 2 + core}

    def y_of(dy):
        return lax.rem(y + dy, RING)

    def at_y(dy):
        return {"col": x_hi * RING + y_of(dy)}

    sibling = {"grp": grp + 1 - 2 * core}
    across = {"col": (1 - x_hi) * RING + y}
    other_chips = [(dz, dx) for dx in (1, 0) for dz in AROUND + [0] if dz or dx]

    loads = [
        pltpu.make_async_copy(src, dst, load_s.at[i])
        for i, (src, dst) in enumerate(
            [(b_hbm, b_ref), (groups_hbm, groups_ref), (panel_hbm, panel_ref), (shift_hbm, shift_ref)])
    ]
    for copy in loads:
        copy.start()

    barrier = pltpu.get_barrier_semaphore()
    peers = [sibling, across] + [at_y(dy) for dy in AROUND] + [at_chip(*step) for step in other_chips]
    for peer in peers:
        pl.semaphore_signal(barrier, 1, device_id=peer, device_id_type=MESH)

    sends = []

    def send(src, dst, s, r, to):
        copy = pltpu.make_async_remote_copy(
            src_ref=src, dst_ref=dst, send_sem=s, recv_sem=r, device_id=to, device_id_type=MESH
        )
        copy.start()
        sends.append(copy)
        return copy

    def arrived(copies):
        for copy in copies:
            copy.wait_recv()

    for copy in loads[1:] + loads[:1]:
        copy.wait()
    owner = panel_ref[0] // 4
    owner_x, owner_y = owner // RING, lax.rem(owner, RING)
    local = lax.rem(panel_ref[0], 4)
    live = groups_ref[grp]
    row = lax.broadcasted_iota(jnp.int32, (GROUP_ROWS, PANEL), 0)
    own[...] = jnp.where(row < live, choose(local, [b_ref[:, k * PANEL : (k + 1) * PANEL] for k in range(4)]), 0.0)

    for k in range(4):
        pack[:, OFFSETS[k] : OFFSETS[k] + PANEL - k * B] = dot(
            own[:, k * B : (k + 1) * B], own[:, k * B :], ((0,), (0,)))
    pl.semaphore_wait(barrier, len(peers))

    half = pl.ds(pl.multiple_of(core * 64, 64), 64)
    half_other = pl.ds(pl.multiple_of((1 - core) * 64, 64), 64)
    swap = send(pack.at[half_other], pack_in, dcore_s, dcore_r, sibling)

    piece = pl.ds(pl.multiple_of(y * PIECE, PIECE), PIECE)
    columns = [pl.ds(h * HALF, HALF) for h in range(2)]
    scatters = [
        [
            send(own.at[pl.ds(pl.multiple_of(y_of(dy) * PIECE, PIECE), PIECE), columns[h]], scat.at[h, y],
                 scat_s.at[h, i], scat_r.at[h, i], at_y(dy))
            for i, dy in enumerate(AROUND)
        ]
        for h in range(2)
    ]
    for h in range(2):
        scat[h, y] = own[piece, h * HALF : (h + 1) * HALF]

    swap.wait_recv()
    pack[half, :] += pack_in[...]
    reduces = [
        send(pack.at[pl.ds(pl.multiple_of(core * 64 + chip_of(*step) * 8, 8), 8)], strips.at[i],
             drs_s.at[i], drs_r.at[i], at_chip(*step))
        for i, step in enumerate(other_chips)
    ]

    def pass_across(h):
        arrived(scatters[h])
        cross[h, x_hi] = choose(owner_y, [scat[h, i] for i in range(RING)])
        return send(cross.at[h, x_hi], cross.at[h, x_hi], cross_s.at[h], cross_r.at[h], across)

    def gather(h):
        crossings[h].wait_recv()
        panel[piece, h * HALF : (h + 1) * HALF] = choose(owner_x, [cross[h, i] for i in range(2)])
        return [
            send(panel.at[piece, columns[h]], panel.at[piece, columns[h]], ag_s.at[h, i], ag_r.at[h, i], at_y(dy))
            for i, dy in enumerate(AROUND)
        ]

    crossings = [pass_across(0)]

    strip_at = pl.multiple_of(core * 64 + (z * 2 + x) * 8, 8)
    strip_rows = pl.ds(strip_at, 8)
    total = pack[strip_rows, :]
    for i, copy in enumerate(reduces):
        copy.wait_recv()
        total += strips[i]
    lane = lax.broadcasted_iota(jnp.int32, (8, B), 1)
    sub = lax.broadcasted_iota(jnp.int32, (8, B), 0)
    for k in range(4):
        terms = choose(local, [shift_ref[:, p * PANEL + k * B : p * PANEL + (k + 1) * B] for p in range(4)])
        terms = jnp.broadcast_to(terms, (8, B))
        strip_y[y, :, OFFSETS[k] : OFFSETS[k] + B] = total[:, OFFSETS[k] : OFFSETS[k] + B] + jnp.where(
            lane == strip_at + sub, terms, 0.0)
        if k < 3:
            strip_y[y, :, OFFSETS[k] + B : OFFSETS[k + 1]] = total[:, OFFSETS[k] + B : OFFSETS[k + 1]]
    spreads = [
        send(strip_y.at[y], strip_y.at[y], dy_s.at[i], dy_r.at[i], at_y(dy)) for i, dy in enumerate(AROUND)
    ]

    crossings.append(pass_across(1))
    gathers = [gather(0)]
    gathers.append(gather(1))

    arrived(spreads)
    strip_x[x_hi] = choose(owner_y, [strip_y[i] for i in range(RING)])
    strip_cross = send(strip_x.at[x_hi], strip_x.at[x_hi], dx_s, dx_r, across)

    strip_cross.wait_recv()
    d_ref[strip_rows, :] = choose(owner_x, [strip_x[c] for c in range(2)])
    parts = [pl.ds(0, B), pl.ds(B, PACKED - B)]
    dgathers = [
        [
            send(d_ref.at[strip_rows, cols], d_ref.at[strip_rows, cols], dag_s.at[p, c], dag_r.at[p, c], at_chip(*chip))
            for c, chip in enumerate(other_chips)
        ]
        for p, cols in enumerate(parts)
    ]

    def to_sibling(p):
        arrived(dgathers[p])
        return send(d_ref.at[half, parts[p]], d_ref.at[half, parts[p]], dsib_s.at[p], dsib_r.at[p], sibling)


    swaps, to_x, to_z = {}, {}, {}

    def gram(h, dz):
        at = pl.multiple_of(lax.rem(z + dz, RING) * 4 * SHARE, 4 * SHARE)
        block = dot(panel_t[h * HALF : (h + 1) * HALF, :], b_ref[:, pl.ds(at, 4 * SHARE)])
        for chip_x in range(2):
            dx = lax.rem(x + chip_x, 2)
            first, second = (block[:, (2 * chip_x + c) * SHARE : (2 * chip_x + c + 1) * SHARE] for c in range(2))
            part[h, dz, dx] = jnp.where(core == 0, first, second)
            other[h, dz, dx] = jnp.where(core == 0, second, first)
        swaps[h, dz] = send(other.at[h, dz], other_in.at[h, dz], core_s.at[h, dz], core_r.at[h, dz], sibling)

    def merge(h, dz):
        swaps[h, dz].wait_recv()
        part[h, dz] += other_in[h, dz]
        if h == 1:
            to_x[dz] = send(part.at[1, dz, 1], first_x.at[dz], fx_s.at[dz], fx_r.at[dz], at_chip(0, 1))
        elif dz:
            to_z[dz] = send(part.at[0, dz], last_z.at[dz], lz_s.at[dz], lz_r.at[dz], at_chip(dz, 0))

    def pass_on_z(dz):
        to_x[dz].wait_recv()
        part[1, dz, 0] += first_x[dz]
        if dz:
            from_z.append(send(part.at[1, dz, 0], first_z.at[dz], fz_s.at[dz], fz_r.at[dz], at_chip(dz, 0)))

    def pass_on_x():
        for dz in AROUND:
            to_z[dz].wait_recv()
            part[0, 0] += last_z[dz]
        return send(part.at[0, 0, 1], last_x, lx_s, lx_r, at_chip(0, 1))

    from_z = []
    order = [(h, dz) for h in range(2) for dz in AROUND + [0]]
    for i, (h, dz) in enumerate(order):
        if i == 4 * h:
            arrived(gathers[h])
            panel_t[h * HALF : (h + 1) * HALF, :] = panel[:, h * HALF : (h + 1) * HALF].T
        gram(h, dz)
        if i >= LAG:
            merge(*order[i - LAG])
    for step in order[-LAG:]:
        merge(*step)
    to_sibling(0).wait_recv()

    first_row = col * WIDTH + grp * SHARE - panel_ref[0] * PANEL
    terms = jnp.broadcast_to(shift_ref[:, pl.ds(pl.multiple_of(grp * SHARE, SHARE), SHARE)], (HALF, SHARE))

    def rows(h, total):
        at_row = h * HALF + lax.broadcasted_iota(jnp.int32, (HALF, SHARE), 0)
        on_diag = first_row + lax.broadcasted_iota(jnp.int32, (HALF, SHARE), 1) == at_row
        total = part[h, 0, 0] + jnp.where(on_diag, terms, 0.0) + total
        return [total[:B, :], total[B:, :]]

    def solved(k, right):
        x_k = dot(inverses[k], right)
        x_ref[:, k * B : (k + 1) * B] = x_k.T
        return x_k

    def under(k, left, right):
        return dot(uppers[k][:, left * B : right * B], x_rows[k], ((0,), (0,)))

    inverses, uppers = [], []
    summed_z = []
    between = {1: lambda: (summed_z.append(pass_on_x()), pass_on_z(3)), 2: lambda: pass_on_z(0)}
    for k in range(4):
        if k == 1:
            pass_on_z(2)
            pass_on_z(1)
        if k == 3:
            summed_z[0].wait_recv()
            upper_rows = rows(0, last_x[...])
            x_rows = [solved(0, upper_rows[0])]
            x_rows.append(solved(1, upper_rows[1] - under(0, 0, 1)))
            carried = under(0, 1, 3) + under(1, 0, 2)
        at = k * B
        if k == 0:
            rest = []
            tiles = [d_ref[8 * i : 8 * i + 8, :B] for i in range(16)]
            tiles = inv_chol(tiles, lambda: rest.append(to_sibling(1)))
            rest[0].wait_recv()
            for r in range(4):
                m_ref[r * B : (r + 1) * B, r * B :] = d_ref[:, OFFSETS[r] : OFFSETS[r] + PANEL - r * B]
        else:
            tiles = inv_chol([m_ref[at + 8 * i : at + 8 * i + 8, at : at + B] for i in range(16)], between.get(k))
        w = jnp.concatenate(tiles, axis=0)
        inverses.append(w)
        if k == 3:
            break
        u = dot(w, m_ref[at : at + B, at + B :])
        uppers.append(u)
        for r in range(k + 1, 4):
            left = u[:, (r - k - 1) * B : (r - k) * B]
            m_ref[r * B : (r + 1) * B, r * B :] -= dot(left, u[:, (r - k - 1) * B :], ((0,), (0,)))
    arrived(from_z)
    lower_rows = rows(1, first_z[1] + first_z[2] + first_z[3])
    x_rows.append(solved(2, lower_rows[0] - carried[:B, :]))
    solved(3, lower_rows[1] - carried[B:, :] - under(2, 0, 1))
    for copy in sends:
        copy.wait_send()


def panel_rows(constraint_rows, shift, group_rows, panel_index):
    f32 = jnp.float32
    dma = pltpu.SemaphoreType.DMA
    buf = lambda *shape: pltpu.VMEM(shape, f32)
    pair = lambda *shape: [dma(*shape) if shape else dma] * 2
    return pl.pallas_call(
        panel_kernel,
        out_shape=jax.ShapeDtypeStruct((SHARE, PANEL), f32),
        in_specs=[pl.BlockSpec(memory_space=pltpu.HBM)] * 4,
        out_specs=pl.BlockSpec(memory_space=pltpu.VMEM),
        scratch_shapes=[
            pltpu.SMEM((16,), jnp.int32),
            pltpu.SMEM((1,), jnp.int32),
            buf(GROUP_ROWS, WIDTH),
            buf(1, WIDTH),
            buf(B, PACKED),
            buf(PANEL, PANEL),
            buf(GROUP_ROWS, PANEL),
            buf(2, RING, PIECE, HALF),
            buf(2, 2, PIECE, HALF),
            buf(GROUP_ROWS, PANEL),
            buf(PANEL, GROUP_ROWS),
            buf(B, PACKED),
            buf(64, PACKED),
            buf(7, 8, PACKED),
            buf(RING, 8, PACKED),
            buf(2, 8, PACKED),
            *[buf(2, RING, 2, HALF, SHARE)] * 3,
            buf(RING, HALF, SHARE),
            buf(RING, HALF, SHARE),
            buf(RING, 2, HALF, SHARE),
            buf(HALF, SHARE),
            dma((4,)),
            *pair((2, 3)), *pair((2,)), *pair((2, 3)), *pair(), *pair((7,)), *pair((3,)), *pair(),
            *pair((2, 7)), *pair((2,)), *pair((2, RING)), *pair((RING,)), *pair((RING,)), *pair((RING,)), *pair(),
        ],
        compiler_params=pltpu.CompilerParams(collective_id=0, has_side_effects=True, vmem_limit_bytes=53 << 20),
    )(group_rows, panel_index, constraint_rows, shift.reshape(1, -1))


def on_device(constraint_rows, shift, group_rows, panel_index):
    return panel_rows(constraint_rows, shift, group_rows, panel_index)


def solution(mesh):
    placed = (P("grp", "col"), P("col"), P(), P())
    return jax.shard_map(
        on_device, mesh=mesh, in_specs=placed, out_specs=P(("col", "grp"), None), check_vma=False
    )
```
